32 devices in a mesh: rep: 4 (over x, core), shard: 4 (over z), ctx: 2 (over y).
Axes of the slice: x: 2, y: 2, z: 4, core: 2. Of those that a mesh axis runs over, the one named last changes fastest.
Arguments:
- tokens: bfloat16 [16, 1024, 512], P(('rep', 'shard'), 'ctx'), may hold values from -6 to 6
- encoded: bfloat16 [16, 512, 512], P(('rep', 'shard'), 'ctx'), may hold values from -6 to 6
- positions: int32 [16, 1024], P(('rep', 'shard'), 'ctx'), may hold values from 0 to 1023, as said below
- bucket_table: int32 [1024], replicated, may hold values from 0 to 31, never falling along the last dimension, each value on 1 to 128 neighbouring positions
- gain_self: bfloat16 [512], P('shard'), may hold values from 0.5 to 1.5
- w_query: bfloat16 [512, 384], P('shard'), may hold values from -0.125 to 0.125
- w_key: bfloat16 [512, 384], P('shard'), may hold values from -0.125 to 0.125
- w_value: bfloat16 [512, 384], P('shard'), may hold values from -0.25 to 0.25
- w_out: bfloat16 [384, 512], P('shard'), may hold values from -1.25 to 1.25
- bias_table: bfloat16 [32, 6], P('shard'), may hold values from -4 to 4
- gain_cross: bfloat16 [512], P('shard'), may hold values from 0.5 to 1.5
- c_query: bfloat16 [512, 384], P('shard'), may hold values from -0.125 to 0.125
- c_key: bfloat16 [512, 384], P('shard'), may hold values from -0.125 to 0.125
- c_value: bfloat16 [512, 384], P('shard'), may hold values from -0.25 to 0.25
- c_out: bfloat16 [384, 512], P('shard'), may hold values from -1.25 to 1.25
- gain_ff: bfloat16 [512], P('shard'), may hold values from 0.5 to 1.5
- w_gate: bfloat16 [512, 1024], P('shard'), may hold values from -0.25 to 0.25
- w_up: bfloat16 [512, 1024], P('shard'), may hold values from -0.25 to 0.25
- w_down: bfloat16 [1024, 512], P('shard'), may hold values from -0.25 to 0.25
- cotangent: bfloat16 [16, 1024, 512], P(('rep', 'shard'), 'ctx'), may hold values from -6 to 6
Outputs:
- layer_output: bfloat16 [16, 1024, 512], P(('rep', 'shard'), 'ctx')
- tokens_grad: float32 [16, 1024, 512], P(('rep', 'shard'), 'ctx')
- encoded_grad: float32 [16, 512, 512], P(('rep', 'shard'), 'ctx')
- grad_gain_self: float32 [512], P('shard')
- grad_w_query: float32 [512, 384], P('shard')
- grad_w_key: float32 [512, 384], P('shard')
- grad_w_value: float32 [512, 384], P('shard')
- grad_w_out: float32 [384, 512], P('shard')
- grad_bias_table: float32 [32, 6], P('shard')
- grad_gain_cross: float32 [512], P('shard')
- grad_c_query: float32 [512, 384], P('shard')
- grad_c_key: float32 [512, 384], P('shard')
- grad_c_value: float32 [512, 384], P('shard')
- grad_c_out: float32 [384, 512], P('shard')
- grad_gain_ff: float32 [512], P('shard')
- grad_w_gate: float32 [512, 1024], P('shard')
- grad_w_up: float32 [512, 1024], P('shard')
- grad_w_down: float32 [1024, 512], P('shard')
The draws below stay inside these ranges and needn't reach their ends.
Inputs may be any that keep to these rules, and one draw needn't show every extreme that they name: In each sequence every position of 0 to 1023 stands in exactly one slot, and each aligned run of 64 slots holds 64 consecutive positions in increasing order. `bucket_table`: never falls as the offset grows; each bucket holds 1 to 128 offsets.
All inputs are finite; a program needn't handle non-finite values.
Results may differ from the reference program's by a relative error of at most 0.033.
The reference program's roundings to bfloat16 on the way count: a program that leaves them out, or rounds other values in their place, can miss the bound.
Values may be sent and summed in bfloat16 or wider, within the bound.
A program may use at most 192 MiB of HBM per device.

```python
import math
import jax
import jax.numpy as jnp
import numpy as np
from jax import lax

D = 512
HEADS = 6
DH = 64
FF = 1024
NB = 32
SEQ_LEN = 1024
ENC_LEN = 512
BLK = 64
INNER = 384
SEQS = 16


def draw_positions(key, part):
    key = jax.random.fold_in(key, 11)
    keys = jax.random.split(key, SEQS)
    order = jax.vmap(lambda single: jax.random.permutation(single, SEQ_LEN // BLK))(keys).astype(jnp.int32)
    within = jnp.arange(BLK, dtype=jnp.int32)
    placed = order[:, :, None] * BLK + within[None, None, :]
    return placed.reshape(SEQS, SEQ_LEN).astype(jnp.int32)


def block_scale(own_key, extent, cuts, low, top_value):
    def one(axis_at, shards_of):
        heights = jax.random.uniform(jax.random.fold_in(jax.random.fold_in(own_key, 6), axis_at), (shards_of,), jnp.float32, low / len(cuts), top_value / len(cuts))
        return jnp.repeat(jnp.exp(heights), extent[axis_at] // shards_of).reshape((-1,) + (1,) * (len(extent) - axis_at - 1))

    loudness = one(*cuts[0])
    for cut in cuts[1:]:
        loudness = loudness * one(*cut)
    return loudness


def profile(number_of, total, bound, slope):
    portions = [(1 << 20) // math.isqrt(standing ** slope) + 1 for standing in range(2, number_of + 1)]
    surplus, counts = total - bound - (number_of - 1), [1] * (number_of - 1)
    while surplus > 0:
        movable = [i for i in range(number_of - 1) if counts[i] < bound]
        mass, left = sum([portions[i] for i in movable]), surplus
        for i in movable:
            addition = min(bound - counts[i], max(1, left * portions[i] // mass), surplus)
            counts[i] = counts[i] + addition
            surplus = surplus - addition
    return np.array([bound] + counts)


def uneven_parts(stream_key, amount, total, most, slope):
    if amount == 2:
        one = jax.random.randint(stream_key, (), max(1, total - most), min(most, total - 1) + 1)
        return jnp.stack([one, total - one])
    sizes = jnp.asarray(profile(amount, total, most, slope), jnp.int32)
    twos = (amount - 1) // 2
    giver, sink = sizes[1:1 + 2 * twos:2], sizes[2:2 + 2 * twos:2]
    room = jnp.minimum(giver - 1, most - sink)
    passed = jax.random.randint(jax.random.fold_in(stream_key, 1), (twos,), 0, 1 << 20) % (room + 1)
    sizes = sizes.at[1:1 + 2 * twos:2].set(giver - passed).at[2:2 + 2 * twos:2].set(sink + passed)
    return sizes[jax.random.permutation(jax.random.fold_in(stream_key, 2), amount)]


def noise(rng, dims, width, reach, cuts=(), held_as=jnp.bfloat16):
    factor_of = block_scale(rng, dims, cuts, -0.22, 0.18) if cuts else 1.0
    values = jax.random.normal(rng, dims, jnp.float32) * width * factor_of
    return jnp.minimum(jnp.maximum(values, -reach), reach).astype(held_as)


def setup_inputs(seed: int = 0) -> dict:
    streams_of = jax.random.split(jax.random.key(seed), 21)
    return {
        "tokens": noise(streams_of[0], (SEQS, SEQ_LEN, D), 1.0, 6.0, ((0, 16), (1, 2))),
        "encoded": noise(streams_of[1], (SEQS, ENC_LEN, D), 1.0, 6.0, ((0, 16), (1, 2))),
        "positions": draw_positions(jax.random.fold_in(streams_of[20], 71), 0),
        "bucket_table": jnp.searchsorted(jnp.cumsum(uneven_parts(streams_of[3], NB, SEQ_LEN, SEQ_LEN // 8, 2)), jnp.arange(SEQ_LEN), side="right").astype(jnp.int32),
        "gain_self": jnp.clip(1.0 + 0.1 * jax.random.normal(streams_of[4], (D,), jnp.float32), 0.5, 1.5).astype(jnp.bfloat16),
        "w_query": noise(streams_of[5], (D, INNER), (4 * D) ** -0.5, 0.125, ((0, 4),)),
        "w_key": noise(streams_of[6], (D, INNER), (4 * D) ** -0.5, 0.125, ((0, 4),)),
        "w_value": noise(streams_of[7], (D, INNER), D ** -0.5, 0.25, ((0, 4),)),
        "w_out": noise(streams_of[8], (INNER, D), (max(INNER * 64 // SEQ_LEN, 8)) ** -0.5, 1.25, ((0, 4),)),
        "bias_table": noise(streams_of[9], (NB, HEADS), 1.0, 4.0, ((0, 4),)),
        "gain_cross": jnp.clip(1.0 + 0.1 * jax.random.normal(streams_of[10], (D,), jnp.float32), 0.5, 1.5).astype(jnp.bfloat16),
        "c_query": noise(streams_of[11], (D, INNER), (4 * D) ** -0.5, 0.125, ((0, 4),)),
        "c_key": noise(streams_of[12], (D, INNER), (4 * D) ** -0.5, 0.125, ((0, 4),)),
        "c_value": noise(streams_of[13], (D, INNER), D ** -0.5, 0.25, ((0, 4),)),
        "c_out": noise(streams_of[14], (INNER, D), (max(INNER * 32 // ENC_LEN, 4)) ** -0.5, 1.25, ((0, 4),)),
        "gain_ff": jnp.clip(1.0 + 0.1 * jax.random.normal(streams_of[15], (D,), jnp.float32), 0.5, 1.5).astype(jnp.bfloat16),
        "w_gate": noise(streams_of[16], (D, FF), D ** -0.5, 0.25, ((0, 4),)),
        "w_up": noise(streams_of[17], (D, FF), D ** -0.5, 0.25, ((0, 4),)),
        "w_down": noise(streams_of[18], (FF, D), (FF // 2) ** -0.5, 0.25, ((0, 4),)),
        "cotangent": noise(streams_of[19], (SEQS, SEQ_LEN, D), 1.0, 6.0, ((0, 16), (1, 2))),
    }


@jax.custom_vjp
def low(v):
    return lax.optimization_barrier(v.astype(jnp.bfloat16)).astype(jnp.float32)

@jax.custom_vjp
def low_back(v):
    return v

def low_keep(v):
    return (low(v), None)

def low_pass(kept, grad):
    return (grad,)

def back_keep(v):
    return (v, None)

def back_low(kept, grad):
    return (low(grad),)
low.defvjp(low_keep, low_pass)
low_back.defvjp(back_keep, back_low)
epsilon = 1e-06
masked_value = -1e+30

def both_ways(value):
    return low(low_back(value))

def rms_norm(inputs, gain):
    return inputs * lax.rsqrt(lax.optimization_barrier(jnp.mean(inputs * inputs, axis=-1, keepdims=True)) + epsilon) * gain

def split_heads(value):
    return value.reshape(value.shape[0], HEADS, DH)

def high_dot(left, right):
    return jnp.dot(left, right, precision=lax.Precision.HIGHEST)

def attend(query, keys, values, bias, causal):
    scores = jnp.einsum('qhd,khd->hqk', split_heads(query), split_heads(keys), precision=lax.Precision.HIGHEST)
    if bias is not None:
        scores = scores + bias
    scores = low_back(scores)
    if causal is not None:
        scores = jnp.where(causal[None], scores, masked_value)
    probs = low(jax.nn.softmax(scores, axis=-1))
    mixed = jnp.einsum('hqk,khd->qhd', probs, split_heads(values), precision=lax.Precision.HIGHEST)
    return mixed.reshape(mixed.shape[0], HEADS * DH)

def layer(inputs, encoder, params, positions, bucket_table):
    gain_self, w_query, w_key, w_value, w_out, bias_table, gain_cross, c_query, c_key, c_value, c_out, gain_ff, w_gate, w_up, w_down = params
    offset = positions[:, None] - positions[None, :]
    causal = offset >= 0
    bucket = bucket_table[jnp.maximum(offset, 0)]
    bias = jnp.transpose(bias_table[bucket], (2, 0, 1))
    hidden_first_layer = low(rms_norm(inputs, gain_self))
    query = both_ways(high_dot(hidden_first_layer, w_query))
    keys = both_ways(high_dot(hidden_first_layer, w_key))
    values = both_ways(high_dot(hidden_first_layer, w_value))
    attn_one = both_ways(attend(query, keys, values, bias, causal))
    after_one = inputs + low_back(high_dot(attn_one, w_out))
    hidden_two = low(rms_norm(after_one, gain_cross))
    cross_q = both_ways(high_dot(hidden_two, c_query))
    cross_k = both_ways(high_dot(encoder, c_key))
    cross_v = both_ways(high_dot(encoder, c_value))
    attn_two = both_ways(attend(cross_q, cross_k, cross_v, None, None))
    after_two = after_one + low_back(high_dot(attn_two, c_out))
    hidden_three = low(rms_norm(after_two, gain_ff))
    gate = low_back(high_dot(hidden_three, w_gate))
    upper = low_back(high_dot(hidden_three, w_up))
    mixed = low(jax.nn.gelu(gate, approximate=True) * upper)
    return after_two + low_back(high_dot(mixed, w_down))

def reference(tokens, encoded, positions, bucket_table, gain_self, w_query, w_key, w_value, w_out, bias_table, gain_cross, c_query, c_key, c_value, c_out, gain_ff, w_gate, w_up, w_down, cotangent):
    params = tuple((p.astype(jnp.float32) for p in (gain_self, w_query, w_key, w_value, w_out, bias_table, gain_cross, c_query, c_key, c_value, c_out, gain_ff, w_gate, w_up, w_down)))

    def one_sequence(totals, item):
        inputs, encoder, slots, cot = item

        def apply(xin, ein, pin):
            return layer(xin, ein, pin, slots, bucket_table)
        result, pull = jax.vjp(apply, inputs, encoder, params)
        input_grad, encoder_grad, param_grads = pull(cot)
        totals = jax.tree.map(lambda acc, new: acc + new, totals, param_grads)
        return (totals, (result.astype(jnp.bfloat16), input_grad, encoder_grad))
    zeros = tuple((jnp.zeros(p.shape, jnp.float32) for p in params))
    grads, (outputs, input_grads, encoder_grads) = lax.scan(one_sequence, zeros, (tokens.astype(jnp.float32), encoded.astype(jnp.float32), positions, cotangent.astype(jnp.float32)))
    return (outputs, input_grads, encoder_grads, grads[0], grads[1], grads[2], grads[3], grads[4], grads[5], grads[6], grads[7], grads[8], grads[9], grads[10], grads[11], grads[12], grads[13], grads[14])
```

```python
import functools

import jax
import jax.numpy as jnp
from jax import lax
from jax.experimental import pallas as pl
from jax.experimental.pallas import tpu as pltpu
from jax.sharding import PartitionSpec as P

HEADS = 6
DH = 64
NB = 32
BLK = 64
SEQ = 1024
LANES = 128
PAIRS = HEADS * DH // LANES

epsilon = 1e-06
masked_value = -1e30


def rms_norm(inputs, gain):
    return inputs * lax.rsqrt(jnp.mean(inputs * inputs, axis=-1, keepdims=True) + epsilon) * gain


def gated_gelu(gate, upper):
    return jax.nn.gelu(gate, approximate=True) * upper


def product(left, right):
    return jnp.dot(left, right, preferred_element_type=jnp.float32)


def left_matrix_product(left, right):
    return lax.dot_general(
        left, right, (((0,), (0,)), ((), ())), preferred_element_type=jnp.float32
    )


def right_product(left, right):
    return lax.dot_general(
        left, right, (((1,), (1,)), ((), ())), preferred_element_type=jnp.float32
    )


def bits_of(size):
    bits, bit = [], 1
    while bit < size:
        bits.append(bit)
        bit *= 2
    return bits


def swap(value, axis, size, bit):
    return lax.ppermute(value, axis, [(i, i ^ bit) for i in range(size)])


def my_bit(axis, bit):
    return (lax.axis_index(axis) // bit) % 2 == 1


def double(value, axis, size, bit, dim=0):
    other = swap(value, axis, size, bit)
    high = my_bit(axis, bit)
    low_part = jnp.where(high, other, value)
    high_part = jnp.where(high, value, other)
    return jnp.concatenate([low_part, high_part], axis=dim)


def halve(value, axis, size, bit, dim=0):
    half = value.shape[dim] // 2
    high = my_bit(axis, bit)
    low_part = lax.slice_in_dim(value, 0, half, axis=dim)
    high_part = lax.slice_in_dim(value, half, 2 * half, axis=dim)
    keep = jnp.where(high, high_part, low_part)
    give = jnp.where(high, low_part, high_part).astype(jnp.bfloat16)
    got = swap(give, axis, size, bit)
    return keep.astype(jnp.float32) + got.astype(jnp.float32)


def gather_axis(value, axis, size):
    for bit in bits_of(size):
        value = double(value, axis, size, bit)
    return value


def reduce_axis(value, axis, size):
    for bit in reversed(bits_of(size)):
        value = halve(value, axis, size, bit)
    return value


def gather_shards(pack, shards, splits):
    piece = pack
    for axis, size, bit in splits:
        half = piece.shape[0] // 2
        piece = jnp.where(my_bit(axis, bit), piece[half:], piece[:half])
    me = lax.axis_index("shard")
    parts = [piece] + [swap(piece, "shard", shards, s) for s in range(1, shards)]
    whole = jnp.zeros((shards,) + piece.shape, piece.dtype)
    for s in range(shards):
        whole = lax.dynamic_update_slice(whole, parts[s][None], (me ^ s, 0, 0))
    for axis, size, bit in reversed(splits):
        whole = double(whole, axis, size, bit, dim=1)
    return whole


def reduce_shards(pack, shards, first, ways):
    val = pack.astype(jnp.bfloat16)
    for axis, size, bit in first:
        val = halve(val, axis, size, bit, dim=1).astype(jnp.bfloat16)
    me = lax.axis_index("shard")
    count = val.shape[1] // len(ways)
    done = []
    for n, way in enumerate(ways):
        part = val[:, n * count : (n + 1) * count]
        for axis, size, bit in way:
            part = halve(part, axis, size, bit, dim=1).astype(jnp.bfloat16)
        total = lax.dynamic_index_in_dim(part, me, 0, keepdims=False).astype(jnp.float32)
        for s in range(1, shards):
            give = lax.dynamic_index_in_dim(part, me ^ s, 0, keepdims=False)
            total = total + swap(give, "shard", shards, s).astype(jnp.float32)
        out = total.astype(jnp.bfloat16)
        for axis, size, bit in reversed(way):
            out = double(out, axis, size, bit)
        done.append(out)
    out = jnp.concatenate(done, axis=0)
    for axis, size, bit in reversed(first):
        out = double(out, axis, size, bit)
    return out


def to_lanes(value):
    count = value.shape[-1] // LANES
    return jnp.concatenate(
        [value[..., i * LANES : (i + 1) * LANES] for i in range(count)], axis=-2
    )


def from_lanes(value, columns):
    count = columns // LANES
    rows = value.shape[-2] // count
    return jnp.concatenate(
        [value[..., i * rows : (i + 1) * rows, :] for i in range(count)], axis=-1
    )


def lane_half(shape):
    return lax.broadcasted_iota(jnp.int32, shape, 1) // DH


def only(value, half, h):
    return jnp.where(half == h, value, jnp.zeros_like(value))


def band_start(block):
    odd = lax.rem(block, 2)
    return odd, pl.multiple_of(SEQ - BLK * block + BLK * odd, LANES)


def self_forward_kernel(all_blk, my_blk, w_ref, q_ref, k_ref, v_ref, o_ref, p_ref, ks, vs, sc, band):
    rows = q_ref.shape[0]
    for b in range(SEQ // BLK):
        at = pl.ds(pl.multiple_of(all_blk[b] * BLK, BLK), BLK)
        ks[at, :] = k_ref[b * BLK : (b + 1) * BLK, :]
        vs[at, :] = v_ref[b * BLK : (b + 1) * BLK, :]
    half = lane_half((rows, LANES))
    outs = []
    for h in range(2):
        line = jnp.broadcast_to(w_ref[h], (BLK, 2 * SEQ))
        line = pltpu.roll(line, 0, 1, stride=1, stride_axis=0)
        band[0] = line
        band[1] = pltpu.roll(line, BLK, 1)
        sc[...] = right_product(only(q_ref[...], half, h), ks[...])

        def body(i, carry):
            at = pl.ds(pl.multiple_of(i * BLK, BLK), BLK)
            odd, start = band_start(my_blk[i])
            s = sc[at, :] + band[odd, :, pl.ds(start, SEQ)]
            e = jnp.exp(s - jnp.max(s, axis=-1, keepdims=True))
            r = 1.0 / jnp.sum(e, axis=-1, keepdims=True)
            p_ref[h, at, :] = (e * r).astype(jnp.bfloat16)
            return carry

        lax.fori_loop(0, rows // BLK, body, 0)
        outs.append(product(p_ref[h], vs[...]))
    o_ref[...] = jnp.where(half == 0, outs[0], outs[1]).astype(jnp.bfloat16)


def self_backward_kernel(
    all_blk, my_blk, q_ref, k_ref, v_ref, do_ref, p_ref, dq_ref, dk_ref, dv_ref, dt_ref, ks, vs, sc, dsc, dks, dvs, band
):
    rows = q_ref.shape[0]
    for b in range(SEQ // BLK):
        at = pl.ds(pl.multiple_of(all_blk[b] * BLK, BLK), BLK)
        ks[at, :] = k_ref[b * BLK : (b + 1) * BLK, :]
        vs[at, :] = v_ref[b * BLK : (b + 1) * BLK, :]
    half = lane_half((rows, LANES))
    khalf = lane_half((SEQ, LANES))
    dqs = []
    for h in range(2):
        sc[...] = right_product(only(do_ref[...], half, h), vs[...])
        band[...] = jnp.zeros_like(band)

        def body(i, carry):
            at = pl.ds(pl.multiple_of(i * BLK, BLK), BLK)
            odd, start = band_start(my_blk[i])
            p = p_ref[h, at, :].astype(jnp.float32)
            dp = sc[at, :]
            ds = (p * (dp - jnp.sum(p * dp, axis=-1, keepdims=True))).astype(jnp.bfloat16)
            dsc[at, :] = ds
            band[odd, :, pl.ds(start, SEQ)] += ds.astype(jnp.float32)
            return carry

        lax.fori_loop(0, rows // BLK, body, 0)
        ds = dsc[...]
        dqs.append(product(ds, ks[...]))
        dk = left_matrix_product(ds, q_ref[...])
        dv = left_matrix_product(p_ref[h], do_ref[...])
        if h == 0:
            dks[...] = dk
            dvs[...] = dv
        else:
            dks[...] = jnp.where(khalf == 0, dks[...], dk)
            dvs[...] = jnp.where(khalf == 0, dvs[...], dv)
        total = band[0] + pltpu.roll(band[1], 2 * SEQ - BLK, 1)
        count = BLK
        while count > 8:
            count //= 2
            total = total[:count] + pltpu.roll(total[count:], 2 * SEQ - count, 1)
        row = lax.broadcasted_iota(jnp.int32, total.shape, 0)
        for bit in (4, 2, 1):
            total = jnp.where((row // bit) % 2 == 1, pltpu.roll(total, 2 * SEQ - bit, 1), total)
        dt_ref[h] = jnp.sum(total, axis=0, keepdims=True)
    dq_ref[...] = jnp.where(half == 0, dqs[0], dqs[1]).astype(jnp.bfloat16)
    for b in range(SEQ // BLK):
        at = pl.ds(pl.multiple_of(all_blk[b] * BLK, BLK), BLK)
        dk_ref[b * BLK : (b + 1) * BLK, :] = dks[at, :].astype(dk_ref.dtype)
        dv_ref[b * BLK : (b + 1) * BLK, :] = dvs[at, :].astype(dv_ref.dtype)


def cross_forward_kernel(q_ref, k_ref, v_ref, o_ref, p_ref):
    half = lane_half(q_ref.shape)
    outs = []
    for h in range(2):
        s = right_product(only(q_ref[...], half, h), k_ref[...])
        e = jnp.exp(s - jnp.max(s, axis=-1, keepdims=True))
        p_ref[h] = (e * (1.0 / jnp.sum(e, axis=-1, keepdims=True))).astype(jnp.bfloat16)
        outs.append(product(p_ref[h], v_ref[...]))
    o_ref[...] = jnp.where(half == 0, outs[0], outs[1]).astype(jnp.bfloat16)


def cross_backward_kernel(q_ref, k_ref, v_ref, do_ref, p_ref, dq_ref, dk_ref, dv_ref):
    half = lane_half(q_ref.shape)
    khalf = lane_half(k_ref.shape)
    dqs, dks, dvs = [], [], []
    for h in range(2):
        dp = right_product(only(do_ref[...], half, h), v_ref[...])
        p = p_ref[h].astype(jnp.float32)
        ds = (p * (dp - jnp.sum(p * dp, axis=-1, keepdims=True))).astype(jnp.bfloat16)
        dqs.append(product(ds, k_ref[...]))
        dks.append(left_matrix_product(ds, q_ref[...]))
        dvs.append(left_matrix_product(p_ref[h], do_ref[...]))
    dq_ref[...] = jnp.where(half == 0, dqs[0], dqs[1]).astype(jnp.bfloat16)
    dk_ref[...] = jnp.where(khalf == 0, dks[0], dks[1]).astype(dk_ref.dtype)
    dv_ref[...] = jnp.where(khalf == 0, dvs[0], dvs[1]).astype(dv_ref.dtype)


def column(rows, shift=0):
    return pl.BlockSpec((rows, LANES), lambda j: (0, j + shift))


def per_pair(*tail):
    return pl.BlockSpec((2,) + tail, lambda j: (j,) + (0,) * len(tail))


def shaped(*shape, dtype=jnp.bfloat16):
    return jax.ShapeDtypeStruct(shape, dtype)


scalars = pl.BlockSpec(memory_space=pltpu.SMEM)
params = pltpu.CompilerParams(vmem_limit_bytes=48 * 1024 * 1024)


def cost(flops, transcendentals=0):
    return pl.CostEstimate(flops=flops, bytes_accessed=16 << 20, transcendentals=transcendentals)


def self_forward(all_blk, my_blk, lines, query, kv):
    rows = query.shape[0]
    return pl.pallas_call(
        self_forward_kernel,
        grid=(PAIRS,),
        in_specs=[scalars, scalars, per_pair(1, 2 * SEQ), column(rows), column(SEQ), column(SEQ, PAIRS)],
        out_specs=[column(rows), per_pair(rows, SEQ)],
        out_shape=[shaped(rows, HEADS * DH), shaped(HEADS, rows, SEQ)],
        scratch_shapes=[
            pltpu.VMEM((SEQ, LANES), jnp.bfloat16),
            pltpu.VMEM((SEQ, LANES), jnp.bfloat16),
            pltpu.VMEM((rows, SEQ), jnp.float32),
            pltpu.VMEM((2, BLK, 2 * SEQ), jnp.float32),
        ],
        compiler_params=params,
        cost_estimate=cost(8 * HEADS * rows * SEQ * DH, HEADS * rows * SEQ),
        name="self_forward",
    )(all_blk, my_blk, lines, query, kv, kv)


def self_backward(all_blk, my_blk, query, kv, dout, probs):
    rows = query.shape[0]
    return pl.pallas_call(
        self_backward_kernel,
        grid=(PAIRS,),
        in_specs=[scalars, scalars, column(rows), column(SEQ), column(SEQ, PAIRS), column(rows), per_pair(rows, SEQ)],
        out_specs=[column(rows), column(SEQ), column(SEQ), per_pair(1, 2 * SEQ)],
        out_shape=[
            shaped(rows, HEADS * DH),
            shaped(SEQ, HEADS * DH),
            shaped(SEQ, HEADS * DH),
            shaped(HEADS, 1, 2 * SEQ, dtype=jnp.float32),
        ],
        scratch_shapes=[
            pltpu.VMEM((SEQ, LANES), jnp.bfloat16),
            pltpu.VMEM((SEQ, LANES), jnp.bfloat16),
            pltpu.VMEM((rows, SEQ), jnp.float32),
            pltpu.VMEM((rows, SEQ), jnp.bfloat16),
            pltpu.VMEM((SEQ, LANES), jnp.float32),
            pltpu.VMEM((SEQ, LANES), jnp.float32),
            pltpu.VMEM((2, BLK, 2 * SEQ), jnp.float32),
        ],
        compiler_params=params,
        cost_estimate=cost(16 * HEADS * rows * SEQ * DH),
        name="self_backward",
    )(all_blk, my_blk, query, kv, kv, dout, probs)


def cross_forward(query, kv):
    rows, length = query.shape[0], kv.shape[0]
    return pl.pallas_call(
        cross_forward_kernel,
        grid=(PAIRS,),
        in_specs=[column(rows), column(length), column(length, PAIRS)],
        out_specs=[column(rows), per_pair(rows, length)],
        out_shape=[shaped(rows, HEADS * DH), shaped(HEADS, rows, length)],
        compiler_params=params,
        cost_estimate=cost(8 * HEADS * rows * length * DH, HEADS * rows * length),
        name="cross_forward",
    )(query, kv, kv)


def cross_backward(query, kv, dout, probs):
    rows, length = query.shape[0], kv.shape[0]
    return pl.pallas_call(
        cross_backward_kernel,
        grid=(PAIRS,),
        in_specs=[column(rows), column(length), column(length, PAIRS), column(rows), per_pair(rows, length)],
        out_specs=[column(rows), column(length), column(length)],
        out_shape=[shaped(rows, HEADS * DH), shaped(length, HEADS * DH), shaped(length, HEADS * DH)],
        compiler_params=params,
        cost_estimate=cost(16 * HEADS * rows * length * DH),
        name="cross_backward",
    )(query, kv, kv, dout, probs)


def local(
    sizes,
    tokens,
    encoded,
    positions,
    bucket_table,
    gain_self,
    w_query,
    w_key,
    w_value,
    w_out,
    bias_table,
    gain_cross,
    c_query,
    c_key,
    c_value,
    c_out,
    gain_ff,
    w_gate,
    w_up,
    w_down,
    cotangent,
):
    reps, shards, ctxs = sizes
    core = [("rep", reps, 1)]
    rest = [("rep", reps, b) for b in bits_of(reps)[1:]]
    across = [("ctx", ctxs, b) for b in bits_of(ctxs)]
    inner = HEADS * DH
    owned_levels = bias_table.shape[0]
    width = tokens.shape[2]

    table_row = jnp.pad(bias_table.reshape(1, -1), ((0, 0), (0, LANES - bias_table.size)))
    small = [g.reshape(-1, LANES) for g in (gain_self, gain_cross, gain_ff)]
    small_rows = small[0].shape[0]
    extra = jnp.pad(
        jnp.concatenate(small + [table_row], axis=0), ((0, 32 - 3 * small_rows - 1), (0, 0))
    )
    early = jnp.concatenate([to_lanes(w) for w in (w_query, w_key, w_value, c_key, c_value)] + [extra])
    early_full = gather_shards(early, shards, core)
    late_names = (w_out, c_query, c_out, w_gate, w_up, w_down)
    late = jnp.concatenate([to_lanes(w) for w in late_names])
    late_full = gather_shards(late, shards, core)

    def unpack(full, shapes):
        outs, at = [], 0
        for rows, columns in shapes:
            count = rows * columns // LANES
            piece = from_lanes(full[:, at : at + count], columns)
            outs.append(piece.reshape(-1, columns))
            at += count
        return outs, at

    (self_query, self_key, self_value, cross_key, cross_value), at = unpack(
        early_full, [w_query.shape] * 5
    )
    gains = [
        early_full[:, at + i * small_rows : at + (i + 1) * small_rows].reshape(-1).astype(jnp.float32)
        for i in range(3)
    ]
    gain_one, gain_two, gain_three = gains
    table_full = early_full[:, at + 3 * small_rows, : bias_table.size].reshape(NB, HEADS)

    inputs = tokens[0].astype(jnp.float32)
    encoder = encoded[0]
    my_blk = positions[0][::BLK] // BLK
    all_blk = gather_axis(my_blk, "ctx", ctxs)
    levels = jnp.arange(NB, dtype=jnp.int32)
    member = (bucket_table[:, None] == levels[None, :]).astype(jnp.float32)
    by_offset = jnp.dot(member, table_full.astype(jnp.float32), precision=lax.Precision.HIGHEST)
    backwards = by_offset.T[:, ::-1]
    lines = jnp.concatenate(
        [
            jnp.full((HEADS, 1), masked_value, jnp.float32),
            backwards,
            jnp.full((HEADS, SEQ - 1), masked_value, jnp.float32),
        ],
        axis=1,
    )[:, None, :]

    hidden_first_layer = rms_norm(inputs, gain_one).astype(jnp.bfloat16)
    self_kv_weight = jnp.concatenate([self_key, self_value], axis=1)
    cross_kv_weight = jnp.concatenate([cross_key, cross_value], axis=1)
    own_kv = product(hidden_first_layer, self_kv_weight).astype(jnp.bfloat16)
    kv = gather_axis(own_kv, "ctx", ctxs)
    query = product(hidden_first_layer, self_query).astype(jnp.bfloat16)
    own_enc_kv = product(encoder, cross_kv_weight).astype(jnp.bfloat16)
    enc_kv = gather_axis(own_enc_kv, "ctx", ctxs)

    attn_one, probs_one = self_forward(all_blk, my_blk, lines, query, kv)

    (self_out, cross_query, cross_out, feed_gate, feed_up, feed_down), unused = unpack(
        late_full, [w.shape for w in late_names]
    )
    after_one = inputs + product(attn_one, self_out)
    hidden_two = rms_norm(after_one, gain_two).astype(jnp.bfloat16)
    cross_q = product(hidden_two, cross_query).astype(jnp.bfloat16)
    attn_two, probs_two = cross_forward(cross_q, enc_kv)
    after_two = after_one + product(attn_two, cross_out)
    hidden_three = rms_norm(after_two, gain_three).astype(jnp.bfloat16)
    gate = product(hidden_three, feed_gate)
    upper = product(hidden_three, feed_up)
    mixed = gated_gelu(gate, upper).astype(jnp.bfloat16)
    decoder_output = (after_two + product(mixed, feed_down)).astype(jnp.bfloat16)

    grad_low = cotangent[0]
    grad_res = grad_low.astype(jnp.float32)
    down_grad = left_matrix_product(mixed, grad_low)
    mixed_grad = right_product(grad_low, feed_down)
    unused, gelu_pull = jax.vjp(gated_gelu, gate, upper)
    gate_grad, upper_grad = gelu_pull(mixed_grad)
    gate_grad = gate_grad.astype(jnp.bfloat16)
    upper_grad = upper_grad.astype(jnp.bfloat16)
    wgate_grad = left_matrix_product(hidden_three, gate_grad)
    wup_grad = left_matrix_product(hidden_three, upper_grad)

    def pack_grads(grads):
        return jnp.concatenate(
            [
                to_lanes(g.astype(jnp.bfloat16).reshape(shards, -1, g.shape[1]))
                for g in grads
            ],
            axis=1,
        )

    ways = [rest + across, across + rest]
    feed_sum = reduce_shards(pack_grads((wgate_grad, wup_grad, down_grad)), shards, core, ways)

    hidden_grad = right_product(gate_grad, feed_gate) + right_product(upper_grad, feed_up)
    unused, norm_pull = jax.vjp(rms_norm, after_two, gain_three)
    back_three, feed_gain_grad = norm_pull(hidden_grad)
    grad_two = grad_res + back_three
    cross_low = grad_two.astype(jnp.bfloat16)
    cross_output_grad = left_matrix_product(attn_two, cross_low)
    attn_two_grad = right_product(cross_low, cross_out).astype(jnp.bfloat16)
    cq_grad, enckey_term, encvalue_term = cross_backward(cross_q, enc_kv, attn_two_grad, probs_two)
    enc_sum = reduce_axis(jnp.concatenate([enckey_term, encvalue_term], axis=1), "ctx", ctxs)
    enc_low = enc_sum.astype(jnp.bfloat16)
    cquery_grad = left_matrix_product(hidden_two, cq_grad)
    hidden_grad = right_product(cq_grad, cross_query)
    unused, norm_pull = jax.vjp(rms_norm, after_one, gain_two)
    back_two, cross_gain_grad = norm_pull(hidden_grad)
    grad_one = grad_two + back_two
    self_low = grad_one.astype(jnp.bfloat16)
    sout_grad = left_matrix_product(attn_one, self_low)
    attn_one_grad = right_product(self_low, self_out).astype(jnp.bfloat16)
    query_grad, key_term, value_term, line_grad = self_backward(
        all_blk, my_blk, query, kv, attn_one_grad, probs_one
    )
    kv_sum = reduce_axis(jnp.concatenate([key_term, value_term], axis=1), "ctx", ctxs)
    kv_low = kv_sum.astype(jnp.bfloat16)

    encoder_grad = right_product(enc_low, cross_kv_weight)
    enc_weight_grad = left_matrix_product(encoder, enc_low)
    squery_grad = left_matrix_product(hidden_first_layer, query_grad)
    kv_weight_grad = left_matrix_product(hidden_first_layer, kv_low)
    hidden_grad = right_product(query_grad, self_query) + right_product(kv_low, self_kv_weight)
    unused, norm_pull = jax.vjp(rms_norm, inputs, gain_one)
    back_one, self_gain_grad = norm_pull(hidden_grad)
    input_grad = grad_one + back_one

    offset_grad = line_grad[:, 0, 1 : SEQ + 1][:, ::-1]
    table_grad = jnp.dot(offset_grad, member, precision=lax.Precision.HIGHEST).T
    small_grads = [
        g.reshape(shards, small_rows, LANES)
        for g in (self_gain_grad, cross_gain_grad, feed_gain_grad)
    ]
    table_rows = table_grad.reshape(shards, 1, -1)
    table_rows = jnp.pad(table_rows, ((0, 0), (0, 0), (0, LANES - table_rows.shape[2])))
    pad_rows = 8 * reps * ctxs
    small_pack = jnp.concatenate(small_grads + [table_rows], axis=1)
    small_pack = jnp.pad(small_pack, ((0, 0), (0, pad_rows - small_pack.shape[1]), (0, 0)))
    attn_pack = jnp.concatenate(
        [
            pack_grads((squery_grad, kv_weight_grad, sout_grad, cquery_grad, enc_weight_grad, cross_output_grad)),
            small_pack.astype(jnp.bfloat16),
        ],
        axis=1,
    )
    attn_sum = reduce_shards(attn_pack, shards, core, ways)

    def unpack_sum(total, shapes):
        outs, at = [], 0
        for rows, columns in shapes:
            count = rows * columns // LANES
            outs.append(from_lanes(total[at : at + count], columns).astype(jnp.float32))
            at += count
        return outs, at

    (g_gate, g_up, g_down), unused = unpack_sum(feed_sum, [w_gate.shape, w_up.shape, w_down.shape])
    own = width // shards
    (g_query, g_kv, g_out, g_cquery, g_enc, g_cout), at = unpack_sum(
        attn_sum,
        [w_query.shape, (own, 2 * inner), w_out.shape, c_query.shape, (own, 2 * inner), c_out.shape],
    )
    tail = attn_sum[at:].astype(jnp.float32)
    g_gains = [tail[i * small_rows : (i + 1) * small_rows].reshape(-1) for i in range(3)]
    g_table = tail[3 * small_rows, : bias_table.size].reshape(owned_levels, HEADS)
    return (
        decoder_output[None],
        input_grad[None],
        encoder_grad[None],
        g_gains[0],
        g_query,
        g_kv[:, :inner],
        g_kv[:, inner:],
        g_out,
        g_table,
        g_gains[1],
        g_cquery,
        g_enc[:, :inner],
        g_enc[:, inner:],
        g_cout,
        g_gains[2],
        g_gate,
        g_up,
        g_down,
    )


def solution(mesh):
    sizes = tuple(mesh.shape[name] for name in ("rep", "shard", "ctx"))
    return jax.shard_map(
        functools.partial(local, sizes),
        mesh=mesh,
        in_specs=(
            P(("rep", "shard"), "ctx", None),
            P(("rep", "shard"), "ctx", None),
            P(("rep", "shard"), "ctx"),
            P(),
            P("shard"),
            P("shard", None),
            P("shard", None),
            P("shard", None),
            P("shard", None),
            P("shard", None),
            P("shard"),
            P("shard", None),
            P("shard", None),
            P("shard", None),
            P("shard", None),
            P("shard"),
            P("shard", None),
            P("shard", None),
            P("shard", None),
            P(("rep", "shard"), "ctx", None),
        ),
        out_specs=(
            P(("rep", "shard"), "ctx", None),
            P(("rep", "shard"), "ctx", None),
            P(("rep", "shard"), "ctx", None),
            P("shard"),
            P("shard", None),
            P("shard", None),
            P("shard", None),
            P("shard", None),
            P("shard", None),
            P("shard"),
            P("shard", None),
            P("shard", None),
            P("shard", None),
            P("shard", None),
            P("shard"),
            P("shard", None),
            P("shard", None),
            P("shard", None),
        ),
        check_vma=False,
    )
```

```python
import functools

import jax
import jax.numpy as jnp
from jax import lax
from jax.experimental import pallas as pl
from jax.experimental.pallas import tpu as pltpu
from jax.sharding import PartitionSpec as P

HEADS = 6
DH = 64
NB = 32
BLK = 64
SEQ = 1024
LANES = 128
PAIRS = HEADS * DH // LANES

epsilon = 1e-06
masked_value = -1e30


def rms_norm(inputs, gain):
    return inputs * lax.rsqrt(jnp.mean(inputs * inputs, axis=-1, keepdims=True) + epsilon) * gain


def gated_gelu(gate, upper):
    return jax.nn.gelu(gate, approximate=True) * upper


def product(left, right):
    return jnp.dot(left, right, preferred_element_type=jnp.float32)


def left_matrix_product(left, right):
    return lax.dot_general(
        left, right, (((0,), (0,)), ((), ())), preferred_element_type=jnp.float32
    )


def right_product(left, right):
    return lax.dot_general(
        left, right, (((1,), (1,)), ((), ())), preferred_element_type=jnp.float32
    )


def bits_of(size):
    bits, bit = [], 1
    while bit < size:
        bits.append(bit)
        bit *= 2
    return bits


def swap(value, axis, size, bit):
    return lax.ppermute(value, axis, [(i, i ^ bit) for i in range(size)])


def my_bit(axis, bit):
    return (lax.axis_index(axis) // bit) % 2 == 1


def double(value, axis, size, bit, dim=0):
    other = swap(value, axis, size, bit)
    high = my_bit(axis, bit)
    low_part = jnp.where(high, other, value)
    high_part = jnp.where(high, value, other)
    return jnp.concatenate([low_part, high_part], axis=dim)


def halve(value, axis, size, bit, dim=0):
    half = value.shape[dim] // 2
    high = my_bit(axis, bit)
    low_part = lax.slice_in_dim(value, 0, half, axis=dim)
    high_part = lax.slice_in_dim(value, half, 2 * half, axis=dim)
    keep = jnp.where(high, high_part, low_part)
    give = jnp.where(high, low_part, high_part).astype(jnp.bfloat16)
    got = swap(give, axis, size, bit)
    return keep.astype(jnp.float32) + got.astype(jnp.float32)


def gather_axis(value, axis, size):
    for bit in bits_of(size):
        value = double(value, axis, size, bit)
    return value


def reduce_axis(value, axis, size):
    for bit in reversed(bits_of(size)):
        value = halve(value, axis, size, bit)
    return value


def gather_shards(pack, shards, splits, after=None):
    piece = pack
    for axis, size, bit in splits:
        half = piece.shape[0] // 2
        piece = jnp.where(my_bit(axis, bit), piece[half:], piece[:half])
    if after is not None:
        piece, unused = lax.optimization_barrier((piece, after))
    me = lax.axis_index("shard")
    parts = [piece] + [swap(piece, "shard", shards, s) for s in range(1, shards)]
    whole = jnp.zeros((shards,) + piece.shape, piece.dtype)
    for s in range(shards):
        whole = lax.dynamic_update_slice(whole, parts[s][None], (me ^ s, 0, 0))
    for axis, size, bit in reversed(splits):
        whole = double(whole, axis, size, bit, dim=1)
    return whole, parts[-1]


class Reduction:
    def __init__(self, pack, shards, first, ways):
        self.val, self.shards, self.first, self.ways = pack, shards, first, ways

    def first_stage(self):
        val = self.val.astype(jnp.bfloat16)
        for axis, size, bit in self.first:
            val = halve(val, axis, size, bit, dim=1).astype(jnp.bfloat16)
        count = val.shape[1] // len(self.ways)
        self.parts = [val[:, n * count : (n + 1) * count] for n in range(len(self.ways))]
        return val

    def across_stage(self, steps):
        for n, way in enumerate(self.ways):
            for axis, size, bit in way[steps]:
                self.parts[n] = halve(self.parts[n], axis, size, bit, dim=1).astype(jnp.bfloat16)
        return self.parts[0]

    def shard_stage(self):
        me = lax.axis_index("shard")
        for n, part in enumerate(self.parts):
            total = lax.dynamic_index_in_dim(part, me, 0, keepdims=False).astype(jnp.float32)
            for s in range(1, self.shards):
                give = lax.dynamic_index_in_dim(part, me ^ s, 0, keepdims=False)
                total = total + swap(give, "shard", self.shards, s).astype(jnp.float32)
            self.parts[n] = total.astype(jnp.bfloat16)
        return self.parts[0]

    def back_stage(self):
        for n, way in enumerate(self.ways):
            for axis, size, bit in reversed(way):
                self.parts[n] = double(self.parts[n], axis, size, bit)
        out = jnp.concatenate(self.parts, axis=0)
        for axis, size, bit in reversed(self.first):
            out = double(out, axis, size, bit)
        return out


def to_lanes(value):
    count = value.shape[-1] // LANES
    return jnp.concatenate(
        [value[..., i * LANES : (i + 1) * LANES] for i in range(count)], axis=-2
    )


def from_lanes(value, columns):
    count = columns // LANES
    rows = value.shape[-2] // count
    return jnp.concatenate(
        [value[..., i * rows : (i + 1) * rows, :] for i in range(count)], axis=-1
    )


def lane_half(shape):
    return lax.broadcasted_iota(jnp.int32, shape, 1) // DH


def only(value, half, h):
    return jnp.where(half == h, value, jnp.zeros_like(value))


def band_start(block):
    odd = lax.rem(block, 2)
    return odd, pl.multiple_of(SEQ - BLK * block + BLK * odd, LANES)


def self_forward_kernel(all_blk, my_blk, w_ref, q_ref, k_ref, v_ref, o_ref, p_ref, ks, vs, sc, band):
    rows = q_ref.shape[0]
    for b in range(SEQ // BLK):
        at = pl.ds(pl.multiple_of(all_blk[b] * BLK, BLK), BLK)
        ks[at, :] = k_ref[b * BLK : (b + 1) * BLK, :]
        vs[at, :] = v_ref[b * BLK : (b + 1) * BLK, :]
    half = lane_half((rows, LANES))
    outs = []
    for h in range(2):
        line = jnp.broadcast_to(w_ref[h], (BLK, 2 * SEQ))
        line = pltpu.roll(line, 0, 1, stride=1, stride_axis=0)
        band[0] = line
        band[1] = pltpu.roll(line, BLK, 1)
        sc[...] = right_product(only(q_ref[...], half, h), ks[...])

        def body(i, carry):
            at = pl.ds(pl.multiple_of(i * BLK, BLK), BLK)
            odd, start = band_start(my_blk[i])
            s = sc[at, :] + band[odd, :, pl.ds(start, SEQ)]
            e = jnp.exp(s - jnp.max(s, axis=-1, keepdims=True))
            r = 1.0 / jnp.sum(e, axis=-1, keepdims=True)
            p_ref[h, at, :] = (e * r).astype(jnp.bfloat16)
            return carry

        lax.fori_loop(0, rows // BLK, body, 0)
        outs.append(product(p_ref[h], vs[...]))
    o_ref[...] = jnp.where(half == 0, outs[0], outs[1]).astype(jnp.bfloat16)


def self_backward_kernel(ties, all_blk, my_blk, q_ref, k_ref, v_ref, do_ref, p_ref, *refs):
    dq_ref, dk_ref, dv_ref, dt_ref, ks, vs, sc, dsc, dks, dvs, band = refs[ties:]
    rows = q_ref.shape[0]
    for b in range(SEQ // BLK):
        at = pl.ds(pl.multiple_of(all_blk[b] * BLK, BLK), BLK)
        ks[at, :] = k_ref[b * BLK : (b + 1) * BLK, :]
        vs[at, :] = v_ref[b * BLK : (b + 1) * BLK, :]
    half = lane_half((rows, LANES))
    khalf = lane_half((SEQ, LANES))
    dqs = []
    for h in range(2):
        sc[...] = right_product(only(do_ref[...], half, h), vs[...])
        band[...] = jnp.zeros_like(band)

        def body(i, carry):
            at = pl.ds(pl.multiple_of(i * BLK, BLK), BLK)
            odd, start = band_start(my_blk[i])
            p = p_ref[h, at, :].astype(jnp.float32)
            dp = sc[at, :]
            ds = (p * (dp - jnp.sum(p * dp, axis=-1, keepdims=True))).astype(jnp.bfloat16)
            dsc[at, :] = ds
            band[odd, :, pl.ds(start, SEQ)] += ds.astype(jnp.float32)
            return carry

        lax.fori_loop(0, rows // BLK, body, 0)
        ds = dsc[...]
        dqs.append(product(ds, ks[...]))
        dk = left_matrix_product(ds, q_ref[...])
        dv = left_matrix_product(p_ref[h], do_ref[...])
        if h == 0:
            dks[...] = dk
            dvs[...] = dv
        else:
            dks[...] = jnp.where(khalf == 0, dks[...], dk)
            dvs[...] = jnp.where(khalf == 0, dvs[...], dv)
        total = band[0] + pltpu.roll(band[1], 2 * SEQ - BLK, 1)
        count = BLK
        while count > 8:
            count //= 2
            total = total[:count] + pltpu.roll(total[count:], 2 * SEQ - count, 1)
        row = lax.broadcasted_iota(jnp.int32, total.shape, 0)
        for bit in (4, 2, 1):
            total = jnp.where((row // bit) % 2 == 1, pltpu.roll(total, 2 * SEQ - bit, 1), total)
        dt_ref[h] = jnp.sum(total, axis=0, keepdims=True)
    dq_ref[...] = jnp.where(half == 0, dqs[0], dqs[1]).astype(jnp.bfloat16)
    for b in range(SEQ // BLK):
        at = pl.ds(pl.multiple_of(all_blk[b] * BLK, BLK), BLK)
        dk_ref[b * BLK : (b + 1) * BLK, :] = dks[at, :].astype(dk_ref.dtype)
        dv_ref[b * BLK : (b + 1) * BLK, :] = dvs[at, :].astype(dv_ref.dtype)


def cross_forward_kernel(q_ref, k_ref, v_ref, o_ref, p_ref):
    half = lane_half(q_ref.shape)
    outs = []
    for h in range(2):
        s = right_product(only(q_ref[...], half, h), k_ref[...])
        e = jnp.exp(s - jnp.max(s, axis=-1, keepdims=True))
        p_ref[h] = (e * (1.0 / jnp.sum(e, axis=-1, keepdims=True))).astype(jnp.bfloat16)
        outs.append(product(p_ref[h], v_ref[...]))
    o_ref[...] = jnp.where(half == 0, outs[0], outs[1]).astype(jnp.bfloat16)


def cross_backward_kernel(q_ref, k_ref, v_ref, do_ref, p_ref, tie_ref, dq_ref, dk_ref, dv_ref):
    half = lane_half(q_ref.shape)
    khalf = lane_half(k_ref.shape)
    dqs, dks, dvs = [], [], []
    for h in range(2):
        dp = right_product(only(do_ref[...], half, h), v_ref[...])
        p = p_ref[h].astype(jnp.float32)
        ds = (p * (dp - jnp.sum(p * dp, axis=-1, keepdims=True))).astype(jnp.bfloat16)
        dqs.append(product(ds, k_ref[...]))
        dks.append(left_matrix_product(ds, q_ref[...]))
        dvs.append(left_matrix_product(p_ref[h], do_ref[...]))
    dq_ref[...] = jnp.where(half == 0, dqs[0], dqs[1]).astype(jnp.bfloat16)
    dk_ref[...] = jnp.where(khalf == 0, dks[0], dks[1]).astype(dk_ref.dtype)
    dv_ref[...] = jnp.where(khalf == 0, dvs[0], dvs[1]).astype(dv_ref.dtype)


def column(rows, shift=0):
    return pl.BlockSpec((rows, LANES), lambda j: (0, j + shift))


def per_pair(*tail):
    return pl.BlockSpec((2,) + tail, lambda j: (j,) + (0,) * len(tail))


def shaped(*shape, dtype=jnp.bfloat16):
    return jax.ShapeDtypeStruct(shape, dtype)


scalars = pl.BlockSpec(memory_space=pltpu.SMEM)
anywhere = pl.BlockSpec(memory_space=pl.ANY)
params = pltpu.CompilerParams(vmem_limit_bytes=48 * 1024 * 1024)


def cost(flops, transcendentals=0):
    return pl.CostEstimate(flops=flops, bytes_accessed=16 << 20, transcendentals=transcendentals)


def self_forward(all_blk, my_blk, lines, query, kv):
    rows = query.shape[0]
    return pl.pallas_call(
        self_forward_kernel,
        grid=(PAIRS,),
        in_specs=[scalars, scalars, per_pair(1, 2 * SEQ), column(rows), column(SEQ), column(SEQ, PAIRS)],
        out_specs=[column(rows), per_pair(rows, SEQ)],
        out_shape=[shaped(rows, HEADS * DH), shaped(HEADS, rows, SEQ)],
        scratch_shapes=[
            pltpu.VMEM((SEQ, LANES), jnp.bfloat16),
            pltpu.VMEM((SEQ, LANES), jnp.bfloat16),
            pltpu.VMEM((rows, SEQ), jnp.float32),
            pltpu.VMEM((2, BLK, 2 * SEQ), jnp.float32),
        ],
        compiler_params=params,
        cost_estimate=cost(8 * HEADS * rows * SEQ * DH, HEADS * rows * SEQ),
        name="self_forward",
    )(all_blk, my_blk, lines, query, kv, kv)


def self_backward(pair, all_blk, my_blk, query, kv, dout, probs, ties):
    rows = query.shape[0]
    specs = [column(rows, pair), column(SEQ, pair), column(SEQ, PAIRS + pair), column(rows, pair)]
    probs_spec = pl.BlockSpec((2, rows, SEQ), lambda j: (j + pair, 0, 0))
    return pl.pallas_call(
        functools.partial(self_backward_kernel, len(ties)),
        grid=(1,),
        in_specs=[scalars, scalars] + specs + [probs_spec] + [anywhere] * len(ties),
        out_specs=[column(rows), column(SEQ), column(SEQ), per_pair(1, 2 * SEQ)],
        out_shape=[
            shaped(rows, LANES),
            shaped(SEQ, LANES),
            shaped(SEQ, LANES),
            shaped(2, 1, 2 * SEQ, dtype=jnp.float32),
        ],
        scratch_shapes=[
            pltpu.VMEM((SEQ, LANES), jnp.bfloat16),
            pltpu.VMEM((SEQ, LANES), jnp.bfloat16),
            pltpu.VMEM((rows, SEQ), jnp.float32),
            pltpu.VMEM((rows, SEQ), jnp.bfloat16),
            pltpu.VMEM((SEQ, LANES), jnp.float32),
            pltpu.VMEM((SEQ, LANES), jnp.float32),
            pltpu.VMEM((2, BLK, 2 * SEQ), jnp.float32),
        ],
        compiler_params=params,
        cost_estimate=cost(16 * 2 * rows * SEQ * DH),
        name="self_backward",
    )(all_blk, my_blk, query, kv, kv, dout, probs, *ties)


def cross_forward(query, kv):
    rows, length = query.shape[0], kv.shape[0]
    return pl.pallas_call(
        cross_forward_kernel,
        grid=(PAIRS,),
        in_specs=[column(rows), column(length), column(length, PAIRS)],
        out_specs=[column(rows), per_pair(rows, length)],
        out_shape=[shaped(rows, HEADS * DH), shaped(HEADS, rows, length)],
        compiler_params=params,
        cost_estimate=cost(8 * HEADS * rows * length * DH, HEADS * rows * length),
        name="cross_forward",
    )(query, kv, kv)


def cross_backward(query, kv, dout, probs, tie):
    rows, length = query.shape[0], kv.shape[0]
    return pl.pallas_call(
        cross_backward_kernel,
        grid=(PAIRS,),
        in_specs=[column(rows), column(length), column(length, PAIRS), column(rows), per_pair(rows, length), anywhere],
        out_specs=[column(rows), column(length), column(length)],
        out_shape=[shaped(rows, HEADS * DH), shaped(length, HEADS * DH), shaped(length, HEADS * DH)],
        compiler_params=params,
        cost_estimate=cost(16 * HEADS * rows * length * DH),
        name="cross_backward",
    )(query, kv, kv, dout, probs, tie)


def local(
    sizes,
    tokens,
    encoded,
    positions,
    bucket_table,
    gain_self,
    w_query,
    w_key,
    w_value,
    w_out,
    bias_table,
    gain_cross,
    c_query,
    c_key,
    c_value,
    c_out,
    gain_ff,
    w_gate,
    w_up,
    w_down,
    cotangent,
):
    reps, shards, ctxs = sizes
    core = [("rep", reps, 1)]
    rest = [("rep", reps, b) for b in bits_of(reps)[1:]]
    across = [("ctx", ctxs, b) for b in bits_of(ctxs)]
    inner = HEADS * DH
    owned_levels = bias_table.shape[0]
    width = tokens.shape[2]

    table_row = jnp.pad(bias_table.reshape(1, -1), ((0, 0), (0, LANES - bias_table.size)))
    small = [g.reshape(-1, LANES) for g in (gain_self, gain_cross, gain_ff)]
    small_rows = small[0].shape[0]
    extra = jnp.pad(
        jnp.concatenate(small + [table_row], axis=0), ((0, 32 - 3 * small_rows - 1), (0, 0))
    )
    early = jnp.concatenate([to_lanes(w) for w in (w_query, w_key, w_value, c_key, c_value)] + [extra])
    early_full, early_part = gather_shards(early, shards, core + across[:1])
    late_names = (w_out, c_query, c_out, w_gate, w_up, w_down)
    late = jnp.concatenate([to_lanes(w) for w in late_names])
    late_full, unused = gather_shards(late, shards, core + rest[:1], early_part)

    def unpack(full, shapes):
        outs, at = [], 0
        for rows, columns in shapes:
            count = rows * columns // LANES
            piece = from_lanes(full[:, at : at + count], columns)
            outs.append(piece.reshape(-1, columns))
            at += count
        return outs, at

    (self_query, self_key, self_value, cross_key, cross_value), at = unpack(
        early_full, [w_query.shape] * 5
    )
    gains = [
        early_full[:, at + i * small_rows : at + (i + 1) * small_rows].reshape(-1).astype(jnp.float32)
        for i in range(3)
    ]
    gain_one, gain_two, gain_three = gains
    table_full = early_full[:, at + 3 * small_rows, : bias_table.size].reshape(NB, HEADS)

    inputs = tokens[0].astype(jnp.float32)
    encoder = encoded[0]
    my_blk = positions[0][::BLK] // BLK
    all_blk = gather_axis(my_blk, "ctx", ctxs)
    levels = jnp.arange(NB, dtype=jnp.int32)
    member = (bucket_table[:, None] == levels[None, :]).astype(jnp.float32)
    by_offset = jnp.dot(member, table_full.astype(jnp.float32), precision=lax.Precision.HIGHEST)
    backwards = by_offset.T[:, ::-1]
    lines = jnp.concatenate(
        [
            jnp.full((HEADS, 1), masked_value, jnp.float32),
            backwards,
            jnp.full((HEADS, SEQ - 1), masked_value, jnp.float32),
        ],
        axis=1,
    )[:, None, :]

    hidden_first_layer = rms_norm(inputs, gain_one).astype(jnp.bfloat16)
    self_kv_weight = jnp.concatenate([self_key, self_value], axis=1)
    cross_kv_weight = jnp.concatenate([cross_key, cross_value], axis=1)
    own_kv = product(hidden_first_layer, self_kv_weight).astype(jnp.bfloat16)
    kv = gather_axis(own_kv, "ctx", ctxs)
    query = product(hidden_first_layer, self_query).astype(jnp.bfloat16)
    own_enc_kv = product(encoder, cross_kv_weight).astype(jnp.bfloat16)
    enc_kv = gather_axis(own_enc_kv, "ctx", ctxs)

    attn_one, probs_one = self_forward(all_blk, my_blk, lines, query, kv)

    (self_out, cross_query, cross_out, feed_gate, feed_up, feed_down), unused = unpack(
        late_full, [w.shape for w in late_names]
    )
    after_one = inputs + product(attn_one, self_out)
    hidden_two = rms_norm(after_one, gain_two).astype(jnp.bfloat16)
    cross_q = product(hidden_two, cross_query).astype(jnp.bfloat16)
    attn_two, probs_two = cross_forward(cross_q, enc_kv)
    after_two = after_one + product(attn_two, cross_out)
    hidden_three = rms_norm(after_two, gain_three).astype(jnp.bfloat16)
    gate = product(hidden_three, feed_gate)
    upper = product(hidden_three, feed_up)
    mixed = gated_gelu(gate, upper).astype(jnp.bfloat16)
    decoder_output = (after_two + product(mixed, feed_down)).astype(jnp.bfloat16)

    grad_low = cotangent[0]
    grad_res = grad_low.astype(jnp.float32)
    down_grad = left_matrix_product(mixed, grad_low)
    mixed_grad = right_product(grad_low, feed_down)
    unused, gelu_pull = jax.vjp(gated_gelu, gate, upper)
    gate_grad, upper_grad = gelu_pull(mixed_grad)
    gate_grad = gate_grad.astype(jnp.bfloat16)
    upper_grad = upper_grad.astype(jnp.bfloat16)
    wgate_grad = left_matrix_product(hidden_three, gate_grad)
    wup_grad = left_matrix_product(hidden_three, upper_grad)

    def pack_grads(grads):
        return jnp.concatenate(
            [
                to_lanes(g.astype(jnp.bfloat16).reshape(shards, -1, g.shape[1]))
                for g in grads
            ],
            axis=1,
        )

    ways = [rest + across, across + rest]
    feed = Reduction(pack_grads((wgate_grad, wup_grad, down_grad)), shards, core, ways)
    feed_first = feed.first_stage()

    hidden_grad = right_product(gate_grad, feed_gate) + right_product(upper_grad, feed_up)
    unused, norm_pull = jax.vjp(rms_norm, after_two, gain_three)
    back_three, feed_gain_grad = norm_pull(hidden_grad)
    grad_two = grad_res + back_three
    cross_low = grad_two.astype(jnp.bfloat16)
    cross_output_grad = left_matrix_product(attn_two, cross_low)
    attn_two_grad = right_product(cross_low, cross_out).astype(jnp.bfloat16)
    cq_grad, enckey_term, encvalue_term = cross_backward(
        cross_q, enc_kv, attn_two_grad, probs_two, feed_first
    )
    feed_across = feed.across_stage(slice(None))
    enc_sum = reduce_axis(jnp.concatenate([enckey_term, encvalue_term], axis=1), "ctx", ctxs)
    enc_low = enc_sum.astype(jnp.bfloat16)
    cquery_grad = left_matrix_product(hidden_two, cq_grad)
    hidden_grad = right_product(cq_grad, cross_query)
    unused, norm_pull = jax.vjp(rms_norm, after_one, gain_two)
    back_two, cross_gain_grad = norm_pull(hidden_grad)
    grad_one = grad_two + back_two
    self_low = grad_one.astype(jnp.bfloat16)
    sout_grad = left_matrix_product(attn_one, self_low)
    attn_one_grad = right_product(self_low, self_out).astype(jnp.bfloat16)
    enc_weight_grad = left_matrix_product(encoder, enc_low)
    cross_pack = pack_grads((cquery_grad, enc_weight_grad, cross_output_grad))
    cross = Reduction(cross_pack, shards, core, ways)
    operands = (all_blk, my_blk, query, kv, attn_one_grad, probs_one)
    pair_grads = [self_backward(0, *operands, (feed_across,))]
    feed_shard = feed.shard_stage()
    cross_first = cross.first_stage()
    pair_grads.append(self_backward(1, *operands, (pair_grads[0][0], feed_shard, cross_first)))
    cross_across = cross.across_stage(slice(None))
    feed_sum = feed.back_stage()
    pair_grads.append(self_backward(2, *operands, (pair_grads[1][0], cross_across)))
    dqs, dks, dvs, dts = zip(*pair_grads)
    query_grad = jnp.concatenate(dqs, axis=1)
    line_grad = jnp.concatenate(dts, axis=0)
    kv_sum = reduce_axis(jnp.concatenate(dks + dvs, axis=1), "ctx", ctxs)
    cross.shard_stage()
    cross_sum = cross.back_stage()
    kv_low = kv_sum.astype(jnp.bfloat16)

    encoder_grad = right_product(enc_low, cross_kv_weight)
    squery_grad = left_matrix_product(hidden_first_layer, query_grad)
    kv_weight_grad = left_matrix_product(hidden_first_layer, kv_low)
    hidden_grad = right_product(query_grad, self_query) + right_product(kv_low, self_kv_weight)
    unused, norm_pull = jax.vjp(rms_norm, inputs, gain_one)
    back_one, self_gain_grad = norm_pull(hidden_grad)
    input_grad = grad_one + back_one

    offset_grad = line_grad[:, 0, 1 : SEQ + 1][:, ::-1]
    table_grad = jnp.dot(offset_grad, member, precision=lax.Precision.HIGHEST).T
    small_grads = [
        g.reshape(shards, small_rows, LANES)
        for g in (self_gain_grad, cross_gain_grad, feed_gain_grad)
    ]
    table_rows = table_grad.reshape(shards, 1, -1)
    table_rows = jnp.pad(table_rows, ((0, 0), (0, 0), (0, LANES - table_rows.shape[2])))
    pad_rows = 8 * reps * ctxs
    small_pack = jnp.concatenate(small_grads + [table_rows], axis=1)
    small_pack = jnp.pad(small_pack, ((0, 0), (0, pad_rows - small_pack.shape[1]), (0, 0)))
    attn_pack = jnp.concatenate(
        [
            pack_grads((squery_grad, kv_weight_grad, sout_grad)),
            small_pack.astype(jnp.bfloat16),
        ],
        axis=1,
    )
    attn = Reduction(attn_pack, shards, core, ways)
    attn.first_stage()
    attn.across_stage(slice(None))
    attn.shard_stage()
    attn_sum = attn.back_stage()

    def unpack_sum(total, shapes):
        outs, at = [], 0
        for rows, columns in shapes:
            count = rows * columns // LANES
            outs.append(from_lanes(total[at : at + count], columns).astype(jnp.float32))
            at += count
        return outs, at

    (g_gate, g_up, g_down), unused = unpack_sum(feed_sum, [w_gate.shape, w_up.shape, w_down.shape])
    own = width // shards
    (g_cquery, g_enc, g_cout), unused = unpack_sum(
        cross_sum, [c_query.shape, (own, 2 * inner), c_out.shape]
    )
    (g_query, g_kv, g_out), at = unpack_sum(
        attn_sum, [w_query.shape, (own, 2 * inner), w_out.shape]
    )
    tail = attn_sum[at:].astype(jnp.float32)
    g_gains = [tail[i * small_rows : (i + 1) * small_rows].reshape(-1) for i in range(3)]
    g_table = tail[3 * small_rows, : bias_table.size].reshape(owned_levels, HEADS)
    return (
        decoder_output[None],
        input_grad[None],
        encoder_grad[None],
        g_gains[0],
        g_query,
        g_kv[:, :inner],
        g_kv[:, inner:],
        g_out,
        g_table,
        g_gains[1],
        g_cquery,
        g_enc[:, :inner],
        g_enc[:, inner:],
        g_cout,
        g_gains[2],
        g_gate,
        g_up,
        g_down,
    )


def solution(mesh):
    sizes = tuple(mesh.shape[name] for name in ("rep", "shard", "ctx"))
    return jax.shard_map(
        functools.partial(local, sizes),
        mesh=mesh,
        in_specs=(
            P(("rep", "shard"), "ctx", None),
            P(("rep", "shard"), "ctx", None),
            P(("rep", "shard"), "ctx"),
            P(),
            P("shard"),
            P("shard", None),
            P("shard", None),
            P("shard", None),
            P("shard", None),
            P("shard", None),
            P("shard"),
            P("shard", None),
            P("shard", None),
            P("shard", None),
            P("shard", None),
            P("shard"),
            P("shard", None),
            P("shard", None),
            P("shard", None),
            P(("rep", "shard"), "ctx", None),
        ),
        out_specs=(
            P(("rep", "shard"), "ctx", None),
            P(("rep", "shard"), "ctx", None),
            P(("rep", "shard"), "ctx", None),
            P("shard"),
            P("shard", None),
            P("shard", None),
            P("shard", None),
            P("shard", None),
            P("shard", None),
            P("shard"),
            P("shard", None),
            P("shard", None),
            P("shard", None),
            P("shard", None),
            P("shard"),
            P("shard", None),
            P("shard", None),
            P("shard", None),
        ),
        check_vma=False,
    )
```
